512 devices in a mesh: ctx: 8 (over z), exp: 16 (over y_hi, x), rep: 4 (over y_lo, core).
Axes of the slice: x: 4, y: 8 (y_hi: 4, y_lo: 2; y = y_hi * 2 + y_lo), z: 8, core: 2. Of those that a mesh axis runs over, the one named last changes fastest.
Arguments:
- acts: bfloat16 [4096, 2048], P(('ctx', 'exp'), 'rep'), may hold values from -6 to 6
- grad_out: bfloat16 [4096, 2048], P(('ctx', 'exp'), 'rep'), may hold values from -0.59765625 to 0.59765625
- experts_idx: int32 [4096, 8], P(('ctx', 'exp')), may hold values from 0 to 127, all different within a row; in each aligned block of 32 rows (0 to 31, 32 to 63, ...) at most 3 rows name the same one
- gate_prob: bfloat16 [4096, 8], P(('ctx', 'exp')), may hold values from 0.049804688 to 1
- w_gate: bfloat16 [128, 768, 2048], P(('ctx', 'exp'), 'rep'), may hold values from -0.125 to 0.125
- w_up: bfloat16 [128, 768, 2048], P(('ctx', 'exp'), 'rep'), may hold values from -0.125 to 0.125
- w_down: bfloat16 [128, 768, 2048], P(('ctx', 'exp'), 'rep'), may hold values from -0.21875 to 0.21875
Outputs:
- acts_grad: bfloat16 [4096, 2048], P(('ctx', 'exp'), 'rep')
- gate_grad_tok: bfloat16 [4096, 8], P(('ctx', 'exp'))
- w_gate_grad: bfloat16 [128, 768, 2048], P(('ctx', 'exp'), 'rep')
- w_up_grad: bfloat16 [128, 768, 2048], P(('ctx', 'exp'), 'rep')
- w_down_grad: bfloat16 [128, 768, 2048], P(('ctx', 'exp'), 'rep')
The draws below stay inside these ranges and needn't reach their ends.
Inputs may be any that keep to these rules, and one draw needn't show every extreme that they name: `experts_idx`: each row names 8 different experts. Within the rows of one index of ctx+exp (32 aligned rows), no expert is named by more than 3 rows, a bound that some block reaches.
All inputs are finite; a program needn't handle non-finite values.
Results may differ from the reference program's by a relative error of at most 0.012.
Values may be sent and summed in bfloat16 or wider, within the bound.
No kernel may reach another device: no remote copies, remote signals or barrier semaphores. Data moves between devices by JAX's collectives and lax.ppermute only.
A program may use at most 64 MiB of HBM per device.

```python
import math
import jax
import jax.numpy as jnp
import numpy as np
from jax import lax

D = 2048
FF = 768
TOP = 8
TOK_DEV = 32
EXPERTS = 128
TOKENS = 4096
CAP = 3
N_CTX = 8
N_EXP = 16
N_REP = 4


def level_of(own_key, shape, split, smallest, top_value):
    loudness = 1.0
    for position, blocks in split:
        heights = jax.random.uniform(jax.random.fold_in(jax.random.fold_in(own_key, 6), position), (blocks,), jnp.float32, smallest / len(split), top_value / len(split))
        loudness = loudness * jnp.repeat(jnp.exp(heights), shape[position] // blocks).reshape((-1,) + (1,) * (len(shape) - 1 - position))
    return loudness


def assign_block(key, own, number, rows, number_of, top, reach, skew):
    ranking = jax.random.permutation(key, number_of)
    heavy_load, common = shares(number_of, rows * top, reach, skew, True), shares(number_of, rows * top, reach, skew, False)
    places = jnp.arange(number_of)

    def named(lengths, turn):
        used = int((lengths > 0).sum())
        fixed = max(1, used // 4)
        passed = fixed + (places - fixed + turn * (used - fixed)) % max(1, number_of - fixed)
        return jnp.zeros((number_of,), jnp.int32).at[ranking[jnp.where(places < fixed, places, passed)]].set(jnp.asarray(lengths, jnp.int32))

    lengths = jnp.where(number % 4 == 0, named(heavy_load, number // 4), named(common, number - number // 4 - 1))
    mixed = jax.random.permutation(jax.random.fold_in(own, 3), number_of)
    donor, receiver = mixed[0:number_of // 2 * 2:2], mixed[1:number_of // 2 * 2:2]
    slack = jnp.minimum(lengths[donor] - 1, reach - lengths[receiver]) // 2
    slack = jnp.where((donor == ranking[0]) | (receiver == ranking[0]) | (lengths[receiver] == 0), 0, jnp.maximum(slack, 0))
    passed = jax.random.randint(jax.random.fold_in(own, 4), (number_of // 2,), 0, 1 << 20) % (slack + 1)
    lengths = lengths.at[donor].add(-passed).at[receiver].add(passed)
    items = jnp.searchsorted(jnp.cumsum(lengths), jnp.arange(rows * top), side="right").astype(jnp.int32)
    grid = items.reshape(top, rows).T
    grid = grid[jax.random.permutation(jax.random.fold_in(own, 1), rows)]
    turn = jax.random.randint(jax.random.fold_in(own, 2), (rows, 1), 0, top)
    return jnp.take_along_axis(grid, (jnp.arange(top)[None, :] + turn) % top, axis=1)


def shares(number_of, total, limit, lean, full):
    weights = [(1 << 20) // math.isqrt(standing ** lean) + 1 for standing in range(1, number_of + 1)]
    largest = limit if full else min(limit, max(-(-total // number_of), total * weights[0] // sum(weights)))
    least = 1 if total - largest >= number_of - 1 else 0
    given, spare = [largest] + [least] * (number_of - 1), total - largest - least * (number_of - 1)
    while spare > 0:
        movable = [i for i in range(1, number_of) if given[i] < largest] or [i for i in range(1, number_of) if given[i] < limit]
        pool, budget = sum([weights[i] for i in movable]), spare
        for i in movable:
            more = min(limit - given[i], max(1, budget * weights[i] // pool), spare)
            given[i] = given[i] + more
            spare = spare - more
    return np.array(given)


def gaussian(key, shape, deviation, reach, shards=(), kind=jnp.bfloat16):
    factor_of = level_of(key, shape, shards, -0.22, 0.18) if shards else 1.0
    array = jax.random.normal(key, shape, jnp.float32) * deviation * factor_of
    return jnp.minimum(jnp.maximum(array, -reach), reach).astype(kind)


def setup_inputs(seed: int = 0) -> dict:
    keys = jax.random.split(jax.random.key(seed), 8)
    acts = gaussian(keys[0], (TOKENS, D), 1.0, 6.0, ((0, 128), (1, 4)))
    grad_out = gaussian(keys[1], (TOKENS, D), 0.1, 0.59765625, ((0, 128), (1, 4)))
    experts_idx_keys = jax.random.split(jax.random.fold_in(keys[2], 1), TOKENS // TOK_DEV)
    experts_idx_turns = jax.random.permutation(jax.random.fold_in(keys[2], 3), TOKENS // TOK_DEV)
    experts_idx = jax.vmap(lambda own, number: assign_block(jax.random.fold_in(keys[2], 2), own, number, TOK_DEV, EXPERTS, TOP, CAP, 2))(experts_idx_keys, experts_idx_turns).reshape((TOKENS, TOP))
    gate_prob = jnp.clip(jnp.exp(math.log(1.0) - 2.9996462 * jax.random.uniform(keys[3], (TOKENS, TOP), jnp.float32) ** level_of(keys[3], (TOKENS, TOP), ((0, 128),), -0.2, 0.2)), 0.049804688, 1.0).astype(jnp.bfloat16)
    w_gate = gaussian(keys[4], (EXPERTS, FF, D), D ** -0.5, 0.125, ((0, 128), (1, 4)))
    w_up = gaussian(keys[5], (EXPERTS, FF, D), D ** -0.5, 0.125, ((0, 128), (1, 4)))
    w_down = gaussian(keys[6], (EXPERTS, FF, D), FF ** -0.5, 0.21875, ((0, 128), (1, 4)))
    return {"acts": acts, "grad_out": grad_out, "experts_idx": experts_idx, "gate_prob": gate_prob, "w_gate": w_gate, "w_up": w_up, "w_down": w_down}


def expert_pass(rows_acts, rows_grad, rows_gate, gate_w, up_w, down_w):
    pre_gate = jnp.dot(rows_acts, gate_w.T, preferred_element_type=jnp.float32)
    pre_up = jnp.dot(rows_acts, up_w.T, preferred_element_type=jnp.float32)
    sigma = jax.nn.sigmoid(pre_gate)
    swish = pre_gate * sigma
    hidden = (swish * pre_up).astype(jnp.bfloat16)
    expert_out = jnp.dot(hidden, down_w, preferred_element_type=jnp.float32)
    gate_total = jnp.sum(expert_out * rows_grad.astype(jnp.float32), axis=1).astype(jnp.bfloat16)
    scaled_grad = (rows_gate.astype(jnp.float32)[:, None] * rows_grad.astype(jnp.float32)).astype(jnp.bfloat16)
    hidden_grad = jnp.dot(scaled_grad, down_w.T, preferred_element_type=jnp.float32)
    grad_gate_pre = (hidden_grad * pre_up * sigma * (1.0 + pre_gate * (1.0 - sigma))).astype(jnp.bfloat16)
    grad_up_pre = (hidden_grad * swish).astype(jnp.bfloat16)
    down_grad = jnp.dot(hidden.T, scaled_grad, preferred_element_type=jnp.float32).astype(jnp.bfloat16)
    gate_grad = jnp.dot(grad_gate_pre.T, rows_acts, preferred_element_type=jnp.float32).astype(jnp.bfloat16)
    up_grad = jnp.dot(grad_up_pre.T, rows_acts, preferred_element_type=jnp.float32).astype(jnp.bfloat16)
    share = FF // N_REP
    row_terms = jnp.zeros((rows_acts.shape[0], D), jnp.float32)
    for piece in range(N_REP):
        lower = piece * share
        upper = lower + share
        partial_sum = jnp.dot(grad_gate_pre[:, lower:upper], gate_w[lower:upper], preferred_element_type=jnp.float32)
        partial_sum = partial_sum + jnp.dot(grad_up_pre[:, lower:upper], up_w[lower:upper], preferred_element_type=jnp.float32)
        rounded = lax.optimization_barrier(partial_sum.astype(jnp.bfloat16))
        row_terms = row_terms + rounded.astype(jnp.float32)
    return row_terms.astype(jnp.bfloat16), gate_total, gate_grad, up_grad, down_grad


def reference(acts, grad_out, experts_idx, gate_prob, w_gate, w_up, w_down):
    tokens_all = acts.shape[0]
    rows_most = CAP * N_CTX * N_EXP
    acts_pad = jnp.concatenate([acts, jnp.zeros((1, D), jnp.bfloat16)], axis=0)
    grad_pad = jnp.concatenate([grad_out, jnp.zeros((1, D), jnp.bfloat16)], axis=0)

    def visit(carry, inputs):
        expert_id, gate_w, up_w, down_w = inputs
        match = experts_idx == expert_id
        routed = jnp.any(match, axis=1)
        token_gate = jnp.sum(jnp.where(match, gate_prob.astype(jnp.float32), 0.0), axis=1).astype(jnp.bfloat16)
        gate_pad = jnp.concatenate([token_gate, jnp.zeros((1,), jnp.bfloat16)], axis=0)
        rows = jnp.nonzero(routed, size=rows_most, fill_value=tokens_all)[0].astype(jnp.int32)
        row_terms, gate_total, gate_grad, up_grad, down_grad = expert_pass(
            acts_pad[rows], grad_pad[rows], gate_pad[rows], gate_w, up_w, down_w)
        acts_acc = carry[0].at[rows].add(row_terms.astype(jnp.float32), mode="drop")
        gate_row = jnp.zeros((tokens_all + 1,), jnp.float32).at[rows].set(gate_total.astype(jnp.float32))
        gate_acc = carry[1] + jnp.where(match, gate_row[:tokens_all, None], 0.0)
        return (acts_acc, gate_acc), (gate_grad, up_grad, down_grad)

    start = (jnp.zeros((tokens_all, D), jnp.float32), jnp.zeros((tokens_all, TOP), jnp.float32))
    (acts_acc, gate_acc), (gate_grads, up_grads, down_grads) = lax.scan(
        visit, start, (jnp.arange(EXPERTS, dtype=jnp.int32), w_gate, w_up, w_down))
    return acts_acc.astype(jnp.bfloat16), gate_acc.astype(jnp.bfloat16), gate_grads, up_grads, down_grads
```

```python
import jax
import jax.numpy as jnp
from jax import lax
from jax.experimental import pallas as pl
from jax.experimental.pallas import tpu as pltpu
from jax.sharding import PartitionSpec as P

BF16 = jnp.bfloat16
F32 = jnp.float32
LANES = 128
GROUP = ("ctx", "exp")
LAST = (((1,), (1,)), ((), ()))
FIRST = (((0,), (0,)), ((), ()))


def swap(x, bit):
    return lax.ppermute(x, "rep", [(i, i ^ bit) for i in range(lax.axis_size("rep"))])


def expert_kernel(me_ref, own_ref, core_ref, chip_ref, far_ref, wg_ref, wu_ref, wd_ref,
                  keep_ref, send_ref, hid_ref, ggp_ref, gup_ref):
    rows, both = own_ref.shape
    width = both // 2
    me = me_ref[0]
    pre_gate = pre_up = hid_grad = None
    shares = []
    for j, x_ref in enumerate((own_ref, core_ref, chip_ref, far_ref)):
        share = pl.ds(pl.multiple_of((me ^ j) * width, width), width)
        shares.append(share)
        acts = x_ref[:, :width]
        grad = x_ref[:, width:]
        a = lax.dot_general(acts, wg_ref[:, share], LAST, preferred_element_type=F32)
        b = lax.dot_general(acts, wu_ref[:, share], LAST, preferred_element_type=F32)
        c = lax.dot_general(grad, wd_ref[:, share], LAST, preferred_element_type=F32)
        pre_gate = a if j == 0 else pre_gate + a
        pre_up = b if j == 0 else pre_up + b
        hid_grad = c if j == 0 else hid_grad + c
    sigma = jax.nn.sigmoid(pre_gate)
    swish = pre_gate * sigma
    hidden = (swish * pre_up).astype(BF16)
    ggp = (hid_grad * pre_up * sigma * (1.0 + pre_gate * (1.0 - sigma))).astype(BF16)
    gup = (hid_grad * swish).astype(BF16)
    hid_ref[...] = hidden
    ggp_ref[...] = ggp
    gup_ref[...] = gup
    gate = jnp.sum(hidden.astype(F32) * hid_grad, axis=1, keepdims=True)
    count = rows // 3
    lane = lax.broadcasted_iota(jnp.int32, (count, LANES), 1)
    table = jnp.zeros((count, LANES), F32)
    for c in range(3):
        table = jnp.where(lane == c, gate[c * count:(c + 1) * count], table)
    table = table.astype(BF16)
    high = count * LANES // width
    for j, out_ref in enumerate((keep_ref, send_ref, keep_ref, send_ref)):
        terms = jnp.dot(ggp, wg_ref[:, shares[j]], preferred_element_type=F32)
        terms = terms + jnp.dot(gup, wu_ref[:, shares[j]], preferred_element_type=F32)
        out_ref[j // 2, :rows, :] = terms.astype(BF16)
        for q in range(width // LANES):
            out_ref[j // 2, rows:, q * LANES:(q + 1) * LANES] = table[q * high:(q + 1) * high]


def weight_kernel(me_ref, own_ref, core_ref, chip_ref, far_ref, hid_ref, ggp_ref, gup_ref,
                  wg_out, wu_out, wd_out):
    width = own_ref.shape[1] // 2
    me = me_ref[0]
    hid, ggp, gup = hid_ref[...].T, ggp_ref[...].T, gup_ref[...].T
    for j, x_ref in enumerate((own_ref, core_ref, chip_ref, far_ref)):
        share = pl.ds(pl.multiple_of((me ^ j) * width, width), width)
        acts = x_ref[:, :width]
        grad = x_ref[:, width:]
        wg_out[:, share] = jnp.dot(ggp, acts, preferred_element_type=F32).astype(BF16)
        wu_out[:, share] = jnp.dot(gup, acts, preferred_element_type=F32).astype(BF16)
        wd_out[:, share] = jnp.dot(hid, grad, preferred_element_type=F32).astype(BF16)


def call(kernel, outs, flops, moved, *args):
    vmem = pl.BlockSpec(memory_space=pltpu.VMEM)
    smem = pl.BlockSpec(memory_space=pltpu.SMEM)
    return pl.pallas_call(
        kernel,
        out_shape=[jax.ShapeDtypeStruct(s, BF16) for s in outs],
        in_specs=[smem] + [vmem] * (len(args) - 1),
        out_specs=[vmem] * len(outs),
        cost_estimate=pl.CostEstimate(flops=flops, bytes_accessed=moved, transcendentals=0),
        compiler_params=pltpu.CompilerParams(vmem_limit_bytes=40 << 20),
    )(*args)


def body(acts, grad_out, experts_idx, gate_prob, w_gate, w_up, w_down):
    tokens, top = experts_idx.shape
    width = acts.shape[1]
    experts = lax.axis_size(GROUP)
    cap = 3
    rows = cap * experts
    units, features = w_gate.shape[1:]
    me = lax.axis_index("rep").astype(jnp.int32).reshape(1)

    label = jnp.arange(experts, dtype=jnp.int32)
    hit = experts_idx.T[None, :, :] == label[:, None, None]
    named = jnp.any(hit, axis=1)
    earlier = jnp.arange(tokens)[:, None] < jnp.arange(tokens)[None, :]
    rank = jnp.dot(named.astype(BF16), earlier.astype(BF16), preferred_element_type=F32)
    gate_of = jnp.sum(jnp.where(hit, gate_prob.T[None].astype(F32), 0.0), axis=1)
    slot = jnp.where(named, rank, -1.0)
    placed = slot[:, None, :] == jnp.arange(cap, dtype=F32)[None, :, None]
    placing = placed.astype(BF16).reshape(rows, tokens)
    scaling = jnp.where(placed, gate_of[:, None, :], 0.0).astype(BF16).reshape(rows, tokens)
    send = jnp.concatenate(
        [
            jnp.dot(placing, acts, preferred_element_type=F32).astype(BF16),
            jnp.dot(scaling, grad_out, preferred_element_type=F32).astype(BF16),
        ],
        axis=1,
    ).reshape(experts, cap * 2 * width // LANES, LANES)
    got = lax.all_to_all(send, GROUP, split_axis=0, concat_axis=0, tiled=True)
    own = got.reshape(experts, cap, 2 * width).transpose(1, 0, 2).reshape(rows, 2 * width)
    chip = swap(own, 2)
    core = swap(own, 1)
    far = swap(chip, 1)
    pieces = (me, own, core, chip, far)

    wide = rows + experts * LANES // width
    product = 2 * rows * units * features
    keep, away, hid, ggp, gup = call(
        expert_kernel,
        [(2, wide, width)] * 2 + [(rows, units)] * 3,
        5 * product,
        (3 * units + 3 * rows) * features * 2,
        *pieces, w_gate[0], w_up[0], w_down[0],
    )
    near = keep + swap(away, 1)
    total = near[0] + swap(near[1], 2)
    wg_grad, wu_grad, wd_grad = call(
        weight_kernel, [(units, features)] * 3, 3 * product, (3 * units + 2 * rows) * features * 2,
        *pieces, hid, ggp, gup,
    )
    table = jnp.concatenate(
        [total[rows:, q * LANES:(q + 1) * LANES] for q in range(width // LANES)], axis=0
    )
    table = jnp.pad(table, ((0, 0), (0, width - LANES)))
    back = jnp.concatenate([total[:rows].reshape(cap, experts, width), table[None]], axis=0)
    back = lax.all_to_all(back.transpose(1, 0, 2), GROUP, split_axis=0, concat_axis=0, tiled=True)

    acts_grad = lax.dot_general(
        placing, back[:, :cap].reshape(rows, width), FIRST, preferred_element_type=F32
    ).astype(BF16)
    flat = experts_idx.reshape(-1)
    picked = (flat[:, None] == label[None, :]).astype(BF16)
    lines = jnp.dot(picked, back[:, cap, :LANES], preferred_element_type=F32)
    mine = jnp.sum(
        jnp.where(hit, rank[:, None, :], 0.0), axis=0
    ).T.reshape(-1)
    lane = jnp.arange(LANES, dtype=F32)
    gates = jnp.sum(jnp.where(lane[None, :] == mine[:, None], lines, 0.0), axis=1)
    gate_grad = (gates.reshape(tokens, top) / gate_prob.astype(F32)).astype(BF16)
    return (acts_grad, gate_grad, wg_grad[None], wu_grad[None], wd_grad[None])


def solution(mesh):
    rows = P(GROUP, "rep")
    table = P(GROUP, None)
    weight = P(GROUP, "rep", None)
    return jax.shard_map(
        body,
        mesh=mesh,
        in_specs=(rows, rows, table, table, weight, weight, weight),
        out_specs=(rows, table, weight, weight, weight),
        check_vma=False,
    )
```

```python
import jax
import jax.numpy as jnp
from jax import lax
from jax.experimental import pallas as pl
from jax.experimental.pallas import tpu as pltpu
from jax.sharding import PartitionSpec as P

BF16 = jnp.bfloat16
F32 = jnp.float32
LANES = 128
CAP = 3
BLOCK = 16
GROUP = ("ctx", "exp")
LAST = (((1,), (1,)), ((), ()))
FIRST = (((0,), (0,)), ((), ()))


def swap(x, bit):
    return lax.ppermute(x, "rep", [(i, i ^ bit) for i in range(lax.axis_size("rep"))])


def iota(shape, dim):
    return lax.broadcasted_iota(jnp.int32, shape, dim)


def low(x, size):
    return x & (size - 1)


def high(x, size):
    return x >> (size.bit_length() - 1)


def routes(idx, gate, experts, copies):
    top, tokens = idx.shape
    lanes = copies * tokens
    repeat = (low(iota((tokens, lanes), 1), tokens) == iota((tokens, lanes), 0)).astype(F32)
    idx = jnp.dot(idx.astype(F32), repeat, preferred_element_type=F32).astype(jnp.int32)
    gate = jnp.dot(gate.astype(F32), repeat, preferred_element_type=F32)
    label = iota((experts, lanes), 0)
    hits = [idx[k:k + 1] == label for k in range(top)]
    named = jnp.zeros((experts, lanes), F32)
    weight = jnp.zeros((experts, lanes), F32)
    for k in range(top):
        named = jnp.where(hits[k], 1.0, named)
        weight = jnp.where(hits[k], gate[k:k + 1], weight)
    before = iota((lanes, lanes), 0) < low(iota((lanes, lanes), 1), tokens)
    rank = jnp.dot(named.astype(BF16), before.astype(BF16), preferred_element_type=F32)
    slot = jnp.where(named > 0.0, rank, -1.0)
    return hits, slot, weight


def send_kernel(*refs):
    sources, out_ref, code_ref, value_ref, held, made_ref, sems = refs[:4], refs[4], *refs[5:7], refs[7:11], *refs[11:]
    copies_in = [
        pltpu.make_async_copy(source, kept, sems.at[n]) for n, (source, kept) in enumerate(zip(sources, held))
    ]
    for copy in copies_in:
        copy.start()
    for copy in copies_in:
        copy.wait()
    idx_ref, gate_ref, acts_ref, grad_ref = held
    experts = code_ref.shape[0]
    tokens, width = acts_ref.shape
    chunks = width // LANES
    copies = 2 * chunks
    lanes = copies * tokens
    _, slot, weight = routes(idx_ref[...], gate_ref[...], experts, copies)
    chunk = high(iota((experts, lanes), 1), tokens)
    code_ref[...] = jnp.where(slot < 0.0, -1, slot.astype(jnp.int32) * copies + chunk)
    value_ref[...] = jnp.where(chunk < chunks, 1.0, weight)
    parts = [acts_ref[:, q * LANES:(q + 1) * LANES] for q in range(chunks)]
    parts += [grad_ref[:, q * LANES:(q + 1) * LANES] for q in range(chunks)]
    data = jnp.concatenate(parts, axis=0)
    lines = CAP * copies
    size = BLOCK * lines
    line = iota((BLOCK, lines, lanes), 1)
    copies_out = []
    for b in range(experts // BLOCK):
        code = code_ref[b * BLOCK:(b + 1) * BLOCK, :][:, None, :]
        value = value_ref[b * BLOCK:(b + 1) * BLOCK, :][:, None, :]
        place = jnp.where(code == line, value, 0.0).astype(BF16).reshape(size, lanes)
        made_ref[b] = jnp.dot(place, data, preferred_element_type=F32).astype(BF16)
        copies_out.append(
            pltpu.make_async_copy(made_ref.at[b], out_ref.at[b * size:(b + 1) * size, :], sems.at[4 + b])
        )
        copies_out[-1].start()
    for copy in copies_out:
        copy.wait()


def mover():
    lines = CAP * 8
    size = BLOCK * lines
    out, line = iota((size, size), 0), iota((size, size), 1)
    return (low(out, BLOCK) * lines + high(out, BLOCK) == line).astype(BF16)


def unpack(move, raw_ref, out_ref):
    size = move.shape[0]
    chunks = out_ref.shape[1] // LANES
    sources = raw_ref.shape[0] // size * BLOCK
    for b in range(sources // BLOCK):
        made = jnp.dot(move, raw_ref[b * size:(b + 1) * size, :], preferred_element_type=F32).astype(BF16)
        for m in range(size // BLOCK):
            row, lane = m // chunks * sources + b * BLOCK, m % chunks * LANES
            out_ref[row:row + BLOCK, lane:lane + LANES] = made[m * BLOCK:(m + 1) * BLOCK]


def share_of(me, j, width):
    return pl.ds(pl.multiple_of((me ^ j) * width, width), width)


def add_piece(totals, me, j, x_ref, w_refs):
    width = x_ref.shape[1] // 2
    share = share_of(me, j, width)
    sides = (x_ref[:, :width], x_ref[:, :width], x_ref[:, width:])
    new = [lax.dot_general(x, w[:, share], LAST, preferred_element_type=F32) for x, w in zip(sides, w_refs)]
    return new if totals is None else [t + n for t, n in zip(totals, new)]


def first_kernel(me_ref, raw_ref, wg_ref, wu_ref, wd_ref, own_ref, *outs):
    unpack(mover(), raw_ref, own_ref)
    totals = add_piece(None, me_ref[0], 0, own_ref, (wg_ref, wu_ref, wd_ref))
    for out, total in zip(outs, totals):
        out[...] = total


def chip_kernel(me_ref, core_ref, raw_ref, wg_ref, wu_ref, wd_ref, a_ref, b_ref, c_ref, chip_ref, *outs):
    unpack(mover(), raw_ref, chip_ref)
    totals = [a_ref[...], b_ref[...], c_ref[...]]
    totals = add_piece(totals, me_ref[0], 1, core_ref, (wg_ref, wu_ref, wd_ref))
    totals = add_piece(totals, me_ref[0], 2, chip_ref, (wg_ref, wu_ref, wd_ref))
    for out, total in zip(outs, totals):
        out[...] = total


def terms_kernel(me_ref, raw_ref, wg_ref, wu_ref, wd_ref, a_ref, b_ref, c_ref,
                 keep_ref, send_ref, hid_ref, ggp_ref, gup_ref, sum_ref, far_out, far_ref, sem):
    rows, both = far_ref.shape
    width = both // 2
    me = me_ref[0]
    unpack(mover(), raw_ref, far_ref)
    copy = pltpu.make_async_copy(far_ref, far_out, sem)
    copy.start()
    totals = [a_ref[...], b_ref[...], c_ref[...]]
    pre_gate, pre_up, hid_grad = add_piece(totals, me, 3, far_ref, (wg_ref, wu_ref, wd_ref))
    sigma = jax.nn.sigmoid(pre_gate)
    swish = pre_gate * sigma
    hidden = (swish * pre_up).astype(BF16)
    ggp = (hid_grad * pre_up * sigma * (1.0 + pre_gate * (1.0 - sigma))).astype(BF16)
    gup = (hid_grad * swish).astype(BF16)
    hid_ref[...] = hidden
    ggp_ref[...] = ggp
    gup_ref[...] = gup
    gate = jnp.sum(hidden.astype(F32) * hid_grad, axis=1, keepdims=True)
    count = rows // CAP
    lane = iota((count, LANES), 1)
    table = jnp.zeros((count, LANES), F32)
    for c in range(CAP):
        table = jnp.where(lane == c, gate[c * count:(c + 1) * count], table)
    table = table.astype(BF16)
    tall = count * LANES // width
    for q in range(width // LANES):
        sum_ref[:, q * LANES:(q + 1) * LANES] = table[q * tall:(q + 1) * tall]
    for j, out_ref in ((3, send_ref), (2, keep_ref)):
        put_terms(me, j, ggp, gup, wg_ref, wu_ref, sum_ref, out_ref)
    copy.wait()


def put_terms(me, j, ggp, gup, wg_ref, wu_ref, sum_ref, out_ref):
    rows, width = ggp.shape[0], out_ref.shape[1]
    share = share_of(me, j, width)
    terms = jnp.dot(ggp, wg_ref[:, share], preferred_element_type=F32)
    terms = terms + jnp.dot(gup, wu_ref[:, share], preferred_element_type=F32)
    out_ref[:rows, :] = terms.astype(BF16)
    out_ref[rows:, :] = sum_ref[...]


def near_kernel(me_ref, ggp_ref, gup_ref, wg_ref, wu_ref, sum_ref, keep_ref, send_ref):
    for j, out_ref in ((1, send_ref), (0, keep_ref)):
        put_terms(me_ref[0], j, ggp_ref[...], gup_ref[...], wg_ref, wu_ref, sum_ref, out_ref)


def weight_kernel(me_ref, own_ref, core_ref, chip_ref, far_ref, hid_ref, ggp_ref, gup_ref,
                  wg_out, wu_out, wd_out):
    width = own_ref.shape[1] // 2
    hid, ggp, gup = hid_ref[...].T, ggp_ref[...].T, gup_ref[...].T
    for j, x_ref in enumerate((own_ref, core_ref, chip_ref, far_ref)):
        share = share_of(me_ref[0], j, width)
        acts = x_ref[:, :width]
        grad = x_ref[:, width:]
        wg_out[:, share] = jnp.dot(ggp, acts, preferred_element_type=F32).astype(BF16)
        wu_out[:, share] = jnp.dot(gup, acts, preferred_element_type=F32).astype(BF16)
        wd_out[:, share] = jnp.dot(hid, grad, preferred_element_type=F32).astype(BF16)


def back_kernel(sum_ref, core_ref, out_ref):
    wide, width = sum_ref.shape
    chunks = width // LANES
    experts = out_ref.shape[0] // BLOCK
    rows = CAP * experts
    tall = wide - rows
    total = (sum_ref[...].astype(F32) + core_ref[...].astype(F32)).astype(BF16)
    table = [total[rows:, q * LANES:(q + 1) * LANES] for q in range(chunks)]
    size = BLOCK * BLOCK
    taken = (chunks * CAP + 1) * BLOCK
    line = low(iota((size, taken), 0), BLOCK)
    source = high(iota((size, taken), 0), BLOCK)
    wanted = jnp.where(
        line < chunks * CAP,
        (low(line, chunks) * CAP + high(line, chunks)) * BLOCK + source,
        jnp.where(line == chunks * CAP, chunks * CAP * BLOCK + source, -1),
    )
    move = (wanted == iota((size, taken), 1)).astype(BF16)
    for b in range(experts // BLOCK):
        parts = [
            total[c * experts + b * BLOCK:c * experts + (b + 1) * BLOCK, i * LANES:(i + 1) * LANES]
            for i in range(chunks) for c in range(CAP)
        ]
        start = b * BLOCK % tall
        parts.append(table[b * BLOCK // tall][start:start + BLOCK])
        data = jnp.concatenate(parts, axis=0)
        out_ref[b * size:(b + 1) * size, :] = jnp.dot(
            move, data, preferred_element_type=F32
        ).astype(BF16)


def token_kernel(idx_ref, gate_ref, back_ref, acts_ref, gate_out):
    tokens, width = acts_ref.shape
    chunks = width // LANES
    experts = back_ref.shape[0] // BLOCK
    hits, slot, _ = routes(idx_ref[...], gate_ref[...], experts, chunks)
    lanes = chunks * tokens
    code = jnp.where(
        slot < 0.0, -1, slot.astype(jnp.int32) * chunks + high(iota((experts, lanes), 1), tokens)
    )
    line = iota((experts, BLOCK, lanes), 1)
    place = jnp.where(code[:, None, :] == line, 1.0, 0.0).astype(BF16).reshape(experts * BLOCK, lanes)
    back = back_ref[...]
    made = lax.dot_general(place, back, FIRST, preferred_element_type=F32).astype(BF16)
    for q in range(chunks):
        acts_ref[:, q * LANES:(q + 1) * LANES] = made[q * tokens:(q + 1) * tokens]
    spot = iota((experts, experts * BLOCK), 0) * BLOCK + chunks * CAP
    pick = (iota((experts, experts * BLOCK), 1) == spot).astype(BF16)
    sums = jnp.dot(pick, back, preferred_element_type=F32)
    chosen = jnp.zeros((experts, lanes), F32)
    for c in range(CAP):
        chosen = jnp.where(slot == float(c), sums[:, c:c + 1], chosen)
    gates = [jnp.sum(jnp.where(hit, chosen, 0.0), axis=0, keepdims=True) for hit in hits]
    gates = jnp.concatenate(gates, axis=0)[:, :tokens]
    gate_out[...] = (gates / gate_ref[...].astype(F32)).astype(BF16)


VMEM = pl.BlockSpec(memory_space=pltpu.VMEM)
HBM = pl.BlockSpec(memory_space=pltpu.HBM)
SMEM = pl.BlockSpec(memory_space=pltpu.SMEM)


def call(kernel, outs, flops, args, scalars=0, scratch=(), space=VMEM, limit=16, kept=0):
    moved = sum(a.size * a.dtype.itemsize for a in args)
    moved += sum(o.size * o.dtype.itemsize for o in outs)
    return pl.pallas_call(
        kernel,
        out_shape=outs,
        in_specs=[SMEM] * scalars + [space] * (len(args) - scalars),
        out_specs=[space] * (len(outs) - kept) + [HBM] * kept,
        scratch_shapes=list(scratch),
        cost_estimate=pl.CostEstimate(flops=flops, bytes_accessed=moved, transcendentals=0),
        compiler_params=pltpu.CompilerParams(vmem_limit_bytes=limit << 20),
    )(*args)


def shape(dims, dtype=BF16):
    return jax.ShapeDtypeStruct(dims, dtype)


def body(acts, grad_out, experts_idx, gate_prob, w_gate, w_up, w_down):
    tokens, top = experts_idx.shape
    width = acts.shape[1]
    experts = lax.axis_size(GROUP)
    rows = CAP * experts
    units, features = w_gate.shape[1:]
    me = lax.axis_index("rep").astype(jnp.int32).reshape(1)
    weights = (w_gate[0], w_up[0], w_down[0])
    idx, gate = experts_idx.T, gate_prob.T

    lines = CAP * 2 * width // LANES
    lanes = 2 * width // LANES * tokens
    (send,) = call(
        send_kernel, [shape((experts * lines, LANES))], 2 * experts * lines * lanes * LANES,
        (idx, gate, acts, grad_out),
        scratch=(
            pltpu.VMEM((experts, lanes), jnp.int32),
            pltpu.VMEM((experts, lanes), F32),
            pltpu.VMEM(idx.shape, idx.dtype),
            pltpu.VMEM(gate.shape, gate.dtype),
            pltpu.VMEM(acts.shape, BF16),
            pltpu.VMEM(acts.shape, BF16),
            pltpu.VMEM((experts // BLOCK, BLOCK * lines, LANES), BF16),
            pltpu.SemaphoreType.DMA((4 + experts // BLOCK,)),
        ),
        space=HBM, limit=56,
    )
    got = lax.all_to_all(
        send.reshape(experts, lines, LANES), GROUP, split_axis=0, concat_axis=0, tiled=True
    ).reshape(experts * lines, LANES)
    chip_raw = swap(got, 2)
    product = 2 * rows * units * width
    sums = [shape((rows, units), F32)] * 3
    held = shape((rows, 2 * width))
    own, *first = call(first_kernel, [held] + sums, 3 * product, (me, got, *weights), 1)
    core = swap(own, 1)
    chip_raw, *first = lax.optimization_barrier((chip_raw, *first))
    far_raw = swap(chip_raw, 1)
    chip, *third = call(
        chip_kernel, [held] + sums, 6 * product, (me, core, chip_raw, *weights, *first), 1
    )
    tall = experts * LANES // width
    piece = shape((rows + tall, width))
    keep2, send3, hid, ggp, gup, gates, far = call(
        terms_kernel, [piece] * 2 + [shape((rows, units))] * 3 + [shape((tall, width)), held], 7 * product,
        (me, far_raw, *weights, *third), 1,
        scratch=(pltpu.VMEM((rows, 2 * width), BF16), pltpu.SemaphoreType.DMA(())), kept=1,
    )
    half = keep2 + swap(send3, 1)
    came = swap(half, 2)
    keep0, send1 = call(near_kernel, [piece] * 2, 4 * product, (me, ggp, gup, *weights[:2], gates), 1)
    near = swap(send1, 1)
    wg_grad, wu_grad, wd_grad = call(
        weight_kernel, [shape((units, features))] * 3, 12 * product,
        (me, own, core, chip, far, hid, ggp, gup), 1,
    )
    (back,) = call(
        back_kernel, [shape((experts * BLOCK, LANES))], 2 * experts * BLOCK * 256 * LANES,
        (keep0 + came, near),
    )
    back = lax.all_to_all(
        back.reshape(experts, BLOCK, LANES), GROUP, split_axis=0, concat_axis=0, tiled=True
    )
    acts_grad, gate_grad = call(
        token_kernel, [shape((tokens, width)), shape((top, tokens))],
        4 * experts * BLOCK * LANES * LANES,
        (idx, gate, back.reshape(experts * BLOCK, LANES)),
    )
    return (acts_grad, gate_grad.T, wg_grad[None], wu_grad[None], wd_grad[None])


def solution(mesh):
    rows = P(GROUP, "rep")
    table = P(GROUP, None)
    weight = P(GROUP, "rep", None)
    return jax.shard_map(
        body,
        mesh=mesh,
        in_specs=(rows, rows, table, table, weight, weight, weight),
        out_specs=(rows, table, weight, weight, weight),
        check_vma=False,
    )
```

```python
import jax
import jax.numpy as jnp
from jax import lax
from jax.experimental import pallas as pl
from jax.experimental.pallas import tpu as pltpu
from jax.sharding import PartitionSpec as P

BF16 = jnp.bfloat16
F32 = jnp.float32
LANES = 128
CAP = 3
BLOCK = 16
GROUP = ("ctx", "exp")
LAST = (((1,), (1,)), ((), ()))
FIRST = (((0,), (0,)), ((), ()))


def swap(x, bit):
    return lax.ppermute(x, "rep", [(i, i ^ bit) for i in range(lax.axis_size("rep"))])


def iota(shape, dim):
    return lax.broadcasted_iota(jnp.int32, shape, dim)


def low(x, size):
    return x & (size - 1)


def high(x, size):
    return x >> (size.bit_length() - 1)


def routes(idx, gate, experts, copies):
    top, tokens = idx.shape
    lanes = copies * tokens
    repeat = (low(iota((tokens, lanes), 1), tokens) == iota((tokens, lanes), 0)).astype(F32)
    idx = jnp.dot(idx.astype(F32), repeat, preferred_element_type=F32).astype(jnp.int32)
    gate = jnp.dot(gate.astype(F32), repeat, preferred_element_type=F32)
    label = iota((experts, lanes), 0)
    hits = [idx[k:k + 1] == label for k in range(top)]
    named = jnp.zeros((experts, lanes), F32)
    weight = jnp.zeros((experts, lanes), F32)
    for k in range(top):
        named = jnp.where(hits[k], 1.0, named)
        weight = jnp.where(hits[k], gate[k:k + 1], weight)
    before = iota((lanes, lanes), 0) < low(iota((lanes, lanes), 1), tokens)
    rank = jnp.dot(named.astype(BF16), before.astype(BF16), preferred_element_type=F32)
    slot = jnp.where(named > 0.0, rank, -1.0)
    return hits, slot, weight


def send_kernel(*refs):
    sources, out_ref, code_ref, value_ref, held, made_ref, sems = refs[:4], refs[4], *refs[5:7], refs[7:11], *refs[11:]
    copies_in = [
        pltpu.make_async_copy(source, kept, sems.at[n]) for n, (source, kept) in enumerate(zip(sources, held))
    ]
    for copy in copies_in:
        copy.start()
    for copy in copies_in:
        copy.wait()
    idx_ref, gate_ref, acts_ref, grad_ref = held
    experts = code_ref.shape[0]
    tokens, width = acts_ref.shape
    chunks = width // LANES
    copies = 2 * chunks
    lanes = copies * tokens
    _, slot, weight = routes(idx_ref[...], gate_ref[...], experts, copies)
    chunk = high(iota((experts, lanes), 1), tokens)
    code_ref[...] = jnp.where(slot < 0.0, -1, slot.astype(jnp.int32) * copies + chunk)
    value_ref[...] = jnp.where(chunk < chunks, 1.0, weight)
    parts = [acts_ref[:, q * LANES:(q + 1) * LANES] for q in range(chunks)]
    parts += [grad_ref[:, q * LANES:(q + 1) * LANES] for q in range(chunks)]
    data = jnp.concatenate(parts, axis=0)
    lines = CAP * copies
    size = BLOCK * lines
    line = iota((BLOCK, lines, lanes), 1)
    copies_out = []
    for b in range(experts // BLOCK):
        code = code_ref[b * BLOCK:(b + 1) * BLOCK, :][:, None, :]
        value = value_ref[b * BLOCK:(b + 1) * BLOCK, :][:, None, :]
        place = jnp.where(code == line, value, 0.0).astype(BF16).reshape(size, lanes)
        made_ref[b] = jnp.dot(place, data, preferred_element_type=F32).astype(BF16)
        copies_out.append(
            pltpu.make_async_copy(made_ref.at[b], out_ref.at[b * size:(b + 1) * size, :], sems.at[4 + b])
        )
        copies_out[-1].start()
    for copy in copies_out:
        copy.wait()


def mover():
    lines = CAP * 8
    size = BLOCK * lines
    out, line = iota((size, size), 0), iota((size, size), 1)
    return (low(out, BLOCK) * lines + high(out, BLOCK) == line).astype(BF16)


def unpack_kernel(raw_ref, out_ref):
    move = mover()
    size = move.shape[0]
    chunks = out_ref.shape[1] // LANES
    sources = raw_ref.shape[0] // size * BLOCK
    for b in range(0, sources // BLOCK, 2):
        pair = [raw_ref[(b + n) * size:(b + n + 1) * size, :] for n in range(2)]
        made = jnp.dot(move, jnp.concatenate(pair, axis=1), preferred_element_type=F32).astype(BF16)
        for m in range(size // BLOCK):
            for n in range(2):
                row, lane = m // chunks * sources + (b + n) * BLOCK, m % chunks * LANES
                part = made[m * BLOCK:(m + 1) * BLOCK, n * LANES:(n + 1) * LANES]
                out_ref[row:row + BLOCK, lane:lane + LANES] = part


def share_of(me, j, width):
    return pl.ds(pl.multiple_of((me ^ j) * width, width), width)


def add_piece(totals, me, j, x_ref, w_refs):
    width = x_ref.shape[1] // 2
    share = share_of(me, j, width)
    sides = (x_ref[:, :width], x_ref[:, :width], x_ref[:, width:])
    new = [lax.dot_general(x, w[:, share], LAST, preferred_element_type=F32) for x, w in zip(sides, w_refs)]
    return new if totals is None else [t + n for t, n in zip(totals, new)]


def first_kernel(me_ref, own_ref, wg_ref, wu_ref, wd_ref, *outs):
    totals = add_piece(None, me_ref[0], 0, own_ref, (wg_ref, wu_ref, wd_ref))
    for out, total in zip(outs, totals):
        out[...] = total


def second_kernel(me_ref, core_ref, chip_ref, wg_ref, wu_ref, wd_ref, a_ref, b_ref, c_ref, *outs):
    totals = [a_ref[...], b_ref[...], c_ref[...]]
    totals = add_piece(totals, me_ref[0], 1, core_ref, (wg_ref, wu_ref, wd_ref))
    totals = add_piece(totals, me_ref[0], 2, chip_ref, (wg_ref, wu_ref, wd_ref))
    for out, total in zip(outs, totals):
        out[...] = total


def terms_kernel(me_ref, far_ref, wg_ref, wu_ref, wd_ref, a_ref, b_ref, c_ref,
                 keep_ref, send_ref, hid_ref, ggp_ref, gup_ref, sum_ref):
    rows, both = far_ref.shape
    width = both // 2
    me = me_ref[0]
    totals = [a_ref[...], b_ref[...], c_ref[...]]
    pre_gate, pre_up, hid_grad = add_piece(totals, me, 3, far_ref, (wg_ref, wu_ref, wd_ref))
    sigma = jax.nn.sigmoid(pre_gate)
    swish = pre_gate * sigma
    hidden = (swish * pre_up).astype(BF16)
    ggp = (hid_grad * pre_up * sigma * (1.0 + pre_gate * (1.0 - sigma))).astype(BF16)
    gup = (hid_grad * swish).astype(BF16)
    hid_ref[...] = hidden
    ggp_ref[...] = ggp
    gup_ref[...] = gup
    gate = jnp.sum(hidden.astype(F32) * hid_grad, axis=1, keepdims=True)
    count = rows // CAP
    lane = iota((count, LANES), 1)
    table = jnp.zeros((count, LANES), F32)
    for c in range(CAP):
        table = jnp.where(lane == c, gate[c * count:(c + 1) * count], table)
    table = table.astype(BF16)
    tall = count * LANES // width
    for q in range(width // LANES):
        sum_ref[:, q * LANES:(q + 1) * LANES] = table[q * tall:(q + 1) * tall]
    for j, out_ref in ((3, send_ref), (2, keep_ref)):
        put_terms(me, j, ggp, gup, wg_ref, wu_ref, sum_ref, out_ref)


def put_terms(me, j, ggp, gup, wg_ref, wu_ref, sum_ref, out_ref):
    rows, width = ggp.shape[0], out_ref.shape[1]
    share = share_of(me, j, width)
    terms = jnp.dot(ggp, wg_ref[:, share], preferred_element_type=F32)
    terms = terms + jnp.dot(gup, wu_ref[:, share], preferred_element_type=F32)
    out_ref[:rows, :] = terms.astype(BF16)
    out_ref[rows:, :] = sum_ref[...]


def near_kernel(me_ref, ggp_ref, gup_ref, wg_ref, wu_ref, sum_ref, keep_ref, send_ref):
    for j, out_ref in ((1, send_ref), (0, keep_ref)):
        put_terms(me_ref[0], j, ggp_ref[...], gup_ref[...], wg_ref, wu_ref, sum_ref, out_ref)


def weight_kernel(me_ref, own_ref, core_ref, chip_ref, far_ref, hid_ref, ggp_ref, gup_ref,
                  wg_out, wu_out, wd_out):
    width = own_ref.shape[1] // 2
    hid, ggp, gup = hid_ref[...].T, ggp_ref[...].T, gup_ref[...].T
    for j, x_ref in enumerate((own_ref, core_ref, chip_ref, far_ref)):
        share = share_of(me_ref[0], j, width)
        acts = x_ref[:, :width]
        grad = x_ref[:, width:]
        wg_out[:, share] = jnp.dot(ggp, acts, preferred_element_type=F32).astype(BF16)
        wu_out[:, share] = jnp.dot(gup, acts, preferred_element_type=F32).astype(BF16)
        wd_out[:, share] = jnp.dot(hid, grad, preferred_element_type=F32).astype(BF16)


def back_kernel(sum_ref, core_ref, out_ref, made_ref, sems):
    wide, width = sum_ref.shape
    chunks = width // LANES
    experts = out_ref.shape[0] // BLOCK
    rows = CAP * experts
    tall = wide - rows
    total = (sum_ref[...].astype(F32) + core_ref[...].astype(F32)).astype(BF16)
    table = [total[rows:, q * LANES:(q + 1) * LANES] for q in range(chunks)]
    size = BLOCK * BLOCK
    taken = (chunks * CAP + 1) * BLOCK
    line = low(iota((size, taken), 0), BLOCK)
    source = high(iota((size, taken), 0), BLOCK)
    wanted = jnp.where(
        line < chunks * CAP,
        (low(line, chunks) * CAP + high(line, chunks)) * BLOCK + source,
        jnp.where(line == chunks * CAP, chunks * CAP * BLOCK + source, -1),
    )
    move = (wanted == iota((size, taken), 1)).astype(BF16)
    copies = []
    for b in range(0, experts // BLOCK, 2):
        pair = []
        for d in (b, b + 1):
            parts = [
                total[c * experts + d * BLOCK:c * experts + (d + 1) * BLOCK, i * LANES:(i + 1) * LANES]
                for i in range(chunks) for c in range(CAP)
            ]
            start = d * BLOCK % tall
            parts.append(table[d * BLOCK // tall][start:start + BLOCK])
            pair.append(jnp.concatenate(parts, axis=0))
        made = jnp.dot(
            move, jnp.concatenate(pair, axis=1), preferred_element_type=F32
        ).astype(BF16)
        for n in range(2):
            made_ref[b + n] = made[:, n * LANES:(n + 1) * LANES]
            copies.append(pltpu.make_async_copy(
                made_ref.at[b + n], out_ref.at[(b + n) * size:(b + n + 1) * size, :], sems.at[b + n]
            ))
            copies[-1].start()
    for copy in copies:
        copy.wait()


def place_kernel(idx_ref, gate_ref, place_ref, slot_ref, name_ref):
    top, tokens = idx_ref.shape
    experts, lanes = slot_ref.shape
    chunks = lanes // tokens
    _, slot, _ = routes(idx_ref[...], gate_ref[...], experts, chunks)
    slot_ref[...] = slot
    repeat = (low(iota((tokens, lanes), 1), tokens) == iota((tokens, lanes), 0)).astype(F32)
    name_ref[...] = jnp.dot(idx_ref[...].astype(F32), repeat, preferred_element_type=F32).astype(jnp.int32)
    code = jnp.where(
        slot < 0.0, -1, slot.astype(jnp.int32) * chunks + high(iota((experts, lanes), 1), tokens)
    )
    line = iota((experts, BLOCK, lanes), 1)
    place = jnp.where(code[:, None, :] == line, 1.0, 0.0).reshape(experts * BLOCK, lanes)
    place_ref[:lanes, :] = place.T.astype(BF16)
    spot = iota((experts, experts * BLOCK), 0) * BLOCK + chunks * CAP
    place_ref[lanes:, :] = (iota((experts, experts * BLOCK), 1) == spot).astype(BF16)


def token_kernel(place_ref, slot_ref, name_ref, gate_ref, back_ref, acts_ref, gate_out):
    tokens, width = acts_ref.shape
    chunks = width // LANES
    experts, lanes = slot_ref.shape
    made = jnp.dot(place_ref[...], back_ref[...], preferred_element_type=F32)
    acts = made[:lanes].astype(BF16)
    for q in range(chunks):
        acts_ref[:, q * LANES:(q + 1) * LANES] = acts[q * tokens:(q + 1) * tokens]
    sums = made[lanes:]
    slot = slot_ref[...]
    chosen = jnp.zeros((experts, lanes), F32)
    for c in range(CAP):
        chosen = jnp.where(slot == float(c), sums[:, c:c + 1], chosen)
    label = iota((experts, lanes), 0)
    name = name_ref[...]
    gates = [
        jnp.sum(jnp.where(name[k:k + 1] == label, chosen, 0.0), axis=0, keepdims=True)
        for k in range(name.shape[0])
    ]
    gates = jnp.concatenate(gates, axis=0)[:, :tokens]
    gate_out[...] = (gates / gate_ref[...].astype(F32)).astype(BF16)


VMEM = pl.BlockSpec(memory_space=pltpu.VMEM)
HBM = pl.BlockSpec(memory_space=pltpu.HBM)
SMEM = pl.BlockSpec(memory_space=pltpu.SMEM)


def call(kernel, outs, flops, args, scalars=0, scratch=(), space=VMEM, limit=16, kept=0):
    moved = sum(a.size * a.dtype.itemsize for a in args)
    moved += sum(o.size * o.dtype.itemsize for o in outs)
    return pl.pallas_call(
        kernel,
        out_shape=outs,
        in_specs=[SMEM] * scalars + [space] * (len(args) - scalars),
        out_specs=[space] * (len(outs) - kept) + [HBM] * kept,
        scratch_shapes=list(scratch),
        cost_estimate=pl.CostEstimate(flops=flops, bytes_accessed=moved, transcendentals=0),
        compiler_params=pltpu.CompilerParams(vmem_limit_bytes=limit << 20),
    )(*args)


def shape(dims, dtype=BF16):
    return jax.ShapeDtypeStruct(dims, dtype)


def body(acts, grad_out, experts_idx, gate_prob, w_gate, w_up, w_down):
    tokens, top = experts_idx.shape
    width = acts.shape[1]
    experts = lax.axis_size(GROUP)
    rows = CAP * experts
    units, features = w_gate.shape[1:]
    me = lax.axis_index("rep").astype(jnp.int32).reshape(1)
    weights = (w_gate[0], w_up[0], w_down[0])
    idx, gate = experts_idx.T, gate_prob.T

    lines = CAP * 2 * width // LANES
    lanes = 2 * width // LANES * tokens
    (send,) = call(
        send_kernel, [shape((experts * lines, LANES))], 2 * experts * lines * lanes * LANES,
        (idx, gate, acts, grad_out),
        scratch=(
            pltpu.VMEM((experts, lanes), jnp.int32),
            pltpu.VMEM((experts, lanes), F32),
            pltpu.VMEM(idx.shape, idx.dtype),
            pltpu.VMEM(gate.shape, gate.dtype),
            pltpu.VMEM(acts.shape, BF16),
            pltpu.VMEM(acts.shape, BF16),
            pltpu.VMEM((experts // BLOCK, BLOCK * lines, LANES), BF16),
            pltpu.SemaphoreType.DMA((4 + experts // BLOCK,)),
        ),
        space=HBM, limit=56,
    )
    got = lax.all_to_all(
        send.reshape(experts, lines, LANES), GROUP, split_axis=0, concat_axis=0, tiled=True
    ).reshape(experts * lines, LANES)
    held = shape((rows, 2 * width))
    (own,) = call(unpack_kernel, [held], 2 * rows * 384 * 2 * width, (got,))
    chip = swap(own, 2)
    core = swap(own, 1)
    product = 2 * rows * units * width
    sums = [shape((rows, units), F32)] * 3
    first = call(first_kernel, sums, 3 * product, (me, own, *weights), 1)
    chip, *first = lax.optimization_barrier((chip, *first))
    far = swap(chip, 1)
    second = call(second_kernel, sums, 6 * product, (me, core, chip, *weights, *first), 1)
    tall = experts * LANES // width
    piece = shape((rows + tall, width))
    keep2, send3, hid, ggp, gup, gates = call(
        terms_kernel, [piece] * 2 + [shape((rows, units))] * 3 + [shape((tall, width))], 7 * product,
        (me, far, *weights, *second), 1,
    )
    half = keep2 + swap(send3, 1)
    came = swap(half, 2)
    keep0, send1 = call(near_kernel, [piece] * 2, 4 * product, (me, ggp, gup, *weights[:2], gates), 1)
    near = swap(send1, 1)
    wg_grad, wu_grad, wd_grad = call(
        weight_kernel, [shape((units, features))] * 3, 12 * product,
        (me, own, core, chip, far, hid, ggp, gup), 1,
    )
    summed = keep0 + came
    (back,) = call(
        back_kernel, [shape((experts * BLOCK, LANES))], 2 * experts * BLOCK * 256 * LANES, (summed, near),
        scratch=(
            pltpu.VMEM((experts // BLOCK, BLOCK * BLOCK, LANES), BF16),
            pltpu.SemaphoreType.DMA((experts // BLOCK,)),
        ),
        kept=1,
    )
    idx, gate, _ = lax.optimization_barrier((idx, gate, summed))
    place, slots, names = call(
        place_kernel,
        [
            shape((LANES + experts, experts * BLOCK)), shape((experts, LANES), F32),
            shape((top, LANES), jnp.int32),
        ],
        experts * BLOCK * LANES * 8, (idx, gate),
    )
    back = lax.all_to_all(
        back.reshape(experts, BLOCK, LANES), GROUP, split_axis=0, concat_axis=0, tiled=True
    )
    acts_grad, gate_grad = call(
        token_kernel, [shape((tokens, width)), shape((top, tokens))],
        4 * experts * BLOCK * LANES * LANES,
        (place, slots, names, gate, back.reshape(experts * BLOCK, LANES)),
    )
    return (acts_grad, gate_grad.T, wg_grad[None], wu_grad[None], wd_grad[None])


def solution(mesh):
    rows = P(GROUP, "rep")
    table = P(GROUP, None)
    weight = P(GROUP, "rep", None)
    return jax.shard_map(
        body,
        mesh=mesh,
        in_specs=(rows, rows, table, table, weight, weight, weight),
        out_specs=(rows, table, weight, weight, weight),
        check_vma=False,
    )
```
